256 devices in a mesh: band: 16 (over z, core), grid: 16 (over y, x).
Axes of the slice: x: 4, y: 4, z: 8, core: 2. Of those that a mesh axis runs over, the one named last changes fastest.
Arguments:
- psi: bfloat16 [128, 3145728], P('grid', 'band'), may hold values from -6 to 6
- tiles: bfloat16 [24576, 2, 128, 64], P(('band', 'grid')), may hold values from -0.5 to 0.5
- tile_block: int32 [24576, 2], P(('band', 'grid')), may hold values from 0 to 31, as said below
- couplings: float32 [2, 16, 16], replicated, as said below
- species: int32 [128], P('band'), may hold values from 0 to 1
Outputs:
- applied: bfloat16 [128, 3145728], P('grid', 'band')
The draws below stay inside these ranges and needn't reach their ends.
Inputs may be any that keep to these rules, and one draw needn't show every extreme that they name: `tile_block`: row r lies in slab s = r // 1536; its tiles name blocks s * 2 to (s + 1) * 2 - 1, or, for s > 0, one of the last 1 block of slab s - 1, s * 2 - 1 to s * 2 - 1. `couplings`: each species' matrix is symmetric.
All inputs are finite; a program needn't handle non-finite values.
Results may differ from the reference program's by a relative error of at most 0.0095.
Values may be sent and summed in bfloat16 or wider, within the bound.
No kernel may reach another device: no remote copies, remote signals or barrier semaphores. Data moves between devices by JAX's collectives and lax.ppermute only.
A program may use at most 64 MiB of HBM per device.

```python
import jax
import jax.numpy as jnp
from jax import lax

BANDS = 128
SUB = 96
PER_ROW = 2
TILE = 128
PROJ = 64
ATOM_PROJ = 16
BLK = 2
EDGE = 1
NSPEC = 2
SPLITS = 16
ROWS = 24576
POINTS = 3145728
NBLK = 32
ATOMS = 128


def draw_tile_block(key, part):
    key = jax.random.fold_in(key, 7)
    first, second, third = jax.random.split(key, 3)
    shape = (ROWS, PER_ROW)
    row = lax.broadcasted_iota(jnp.int32, shape, 0)
    slab = row // (SUB * SPLITS)
    own = jax.random.randint(first, shape, 0, BLK, dtype=jnp.int32)
    edge = jax.random.randint(second, shape, 0, EDGE, dtype=jnp.int32)
    pick = jax.random.randint(third, shape, 0, 5, dtype=jnp.int32)
    use_edge = (pick == 0) & (slab > 0)
    return jnp.where(use_edge, slab * BLK - EDGE + edge, slab * BLK + own).astype(jnp.int32)


def draw_couplings(key, part):
    key = jax.random.fold_in(key, 11)
    per_block = SUB * SPLITS * PER_ROW / BLK
    scale = (TILE / (per_block * PER_ROW * PROJ * ATOM_PROJ)) ** 0.5
    shape = (NSPEC, ATOM_PROJ, ATOM_PROJ)
    base = jax.random.normal(key, shape, jnp.float32)
    sym = 0.5 * (base + jnp.swapaxes(base, 1, 2))
    diagonal = jnp.eye(ATOM_PROJ, dtype=jnp.float32)
    return (scale * (sym + 3.0 * diagonal)).astype(jnp.float32)


def plant(drawn, stream_key, least, top_value):
    dims = drawn.shape
    index_at = [jax.random.randint(jax.random.fold_in(stream_key, axis), (), 0, dims[axis]) for axis in range(len(dims))]
    drawn = drawn.at[tuple(index_at)].set(least)
    longest = dims.index(max(dims))
    index_at[longest] = (index_at[longest] + 1) % dims[longest]
    return drawn.at[tuple(index_at)].set(top_value)


def block_scale(own_key, extent, cuts, least, top_value):
    factor_of, own = 1.0, jax.random.fold_in(own_key, 6)
    for dim, parts in cuts:
        heights = jnp.exp(jax.random.uniform(jax.random.fold_in(own, dim), (parts,), jnp.float32, least / len(cuts), top_value / len(cuts)))
        factor_of = factor_of * jnp.repeat(heights, extent[dim] // parts).reshape([-1 if axis == dim else 1 for axis in range(len(extent))])
    return factor_of


def noise(own_key, dims, scale, bound, shards=(), held_as=jnp.bfloat16):
    drawn = scale * jax.random.normal(own_key, dims, jnp.float32)
    if shards:
        drawn = drawn * block_scale(own_key, dims, shards, -0.22, 0.18)
    return jnp.clip(drawn, -bound, bound).astype(held_as)


def setup_inputs(seed: int = 0) -> dict:
    arg_keys = jax.random.split(jax.random.key(seed), 6)
    psi = noise(arg_keys[0], (BANDS, POINTS), 1.0, 6.0, ((0, 16), (1, 16)))
    tiles = noise(arg_keys[1], (ROWS, PER_ROW, TILE, PROJ), TILE ** -0.5, 0.5, ((0, 256),))
    tile_block = draw_tile_block(jax.random.fold_in(arg_keys[5], 71), 0)
    couplings = draw_couplings(jax.random.fold_in(arg_keys[5], 71), 0)
    species = plant(jax.random.randint(arg_keys[4], (ATOMS,), 0, NSPEC), jax.random.fold_in(arg_keys[4], 1), 0, NSPEC - 1).astype(jnp.int32)
    return {"psi": psi, "tiles": tiles, "tile_block": tile_block, "couplings": couplings, "species": species}


def couple(blocks, kinds, couplings):
    count, width, depth = blocks.shape
    atom_proj = couplings.shape[1]
    per_atom = blocks.reshape(count * (width // atom_proj), atom_proj, depth)
    table = jnp.zeros((per_atom.shape[0], atom_proj, atom_proj), jnp.float32)
    for kind in range(couplings.shape[0]):
        table = table + jnp.where((kinds == kind)[:, None, None], couplings[kind], jnp.float32(0.0))
    mixed = jnp.einsum("aij,ajn->ain", table, per_atom, precision=lax.Precision.HIGHEST)
    return mixed.reshape(count, width, depth)


def reference(psi, tiles, tile_block, couplings, species):
    points = psi.reshape(BANDS, ROWS, TILE)
    steps = jnp.arange(ROWS // SUB, dtype=jnp.int32)

    def forward(total, index):
        start = (index * SUB).astype(jnp.int32)
        cols = lax.dynamic_slice_in_dim(points, start, SUB, 1).astype(jnp.float32)
        values = lax.dynamic_slice_in_dim(tiles, start, SUB, 0).astype(jnp.float32)
        names = lax.dynamic_slice_in_dim(tile_block, start, SUB, 0)
        part = jnp.einsum("rjip,nri->rjpn", values, cols, precision=lax.Precision.HIGHEST)
        return total.at[names.reshape(-1)].add(part.reshape(-1, PROJ, BANDS)), None

    start_total = jnp.zeros((NBLK, PROJ, BANDS), jnp.float32)
    coefficients, _ = lax.scan(forward, start_total, steps)
    coupled = couple(coefficients, species, couplings).astype(jnp.bfloat16)

    def backward(index):
        start = (index * SUB).astype(jnp.int32)
        values = lax.dynamic_slice_in_dim(tiles, start, SUB, 0).astype(jnp.float32)
        names = lax.dynamic_slice_in_dim(tile_block, start, SUB, 0)
        picked = coupled[names].astype(jnp.float32)
        result = jnp.einsum("rjip,rjpn->nri", values, picked, precision=lax.Precision.HIGHEST)
        return result.astype(jnp.bfloat16)

    pieces = lax.map(backward, steps)
    return jnp.transpose(pieces, (1, 0, 2, 3)).reshape(BANDS, ROWS * TILE)
```

```python
import jax
import jax.numpy as jnp
from jax import lax
from jax.experimental import pallas as pl
from jax.experimental.pallas import tpu as pltpu
from jax.sharding import PartitionSpec as P

BLK = 2
EDGE = 1
SLOTS = BLK + EDGE
VMEM_LIMIT = 48 * 1024 * 1024


def whole(space=pltpu.VMEM):
    return pl.BlockSpec(memory_space=space)


def call(kernel, out_shape, in_spaces, out_spaces, scratch=(), flops=0, moved=0):
    single = not isinstance(out_shape, (tuple, list))
    return pl.pallas_call(
        kernel,
        out_shape=out_shape,
        in_specs=[whole(s) for s in in_spaces],
        out_specs=whole(out_spaces) if single else [whole(s) for s in out_spaces],
        scratch_shapes=list(scratch),
        compiler_params=pltpu.CompilerParams(vmem_limit_bytes=VMEM_LIMIT),
        cost_estimate=pl.CostEstimate(flops=flops, bytes_accessed=moved, transcendentals=0),
    )


def forward_kernel(slots_ref, columns_ref, tiles_ref, own_ref, edge_ref, total):
    rows, per_row, proj, tile = tiles_ref.shape
    groups, local, _ = columns_ref.shape
    bands = groups * local
    total[...] = jnp.zeros_like(total)

    def row(r, carry):
        at = pl.ds(pl.multiple_of(r * tile, tile), tile)
        columns = columns_ref[:, :, at].reshape(bands, tile)
        values = tiles_ref[r].reshape(per_row * proj, tile)
        part = lax.dot_general(
            values, columns, (((1,), (1,)), ((), ())), preferred_element_type=jnp.float32
        )
        for j in range(per_row):
            total[slots_ref[r, j]] += part[j * proj : (j + 1) * proj]
        return carry

    lax.fori_loop(0, rows, row, 0, unroll=8)
    own_ref[...] = total[EDGE:].reshape(own_ref.shape)
    edge_ref[...] = total[0].astype(edge_ref.dtype)


def couple_kernel(parts_ref, mix_ref, coupled_ref):
    count = parts_ref.shape[0]
    summed = parts_ref[0].astype(jnp.float32)
    for source in range(1, count):
        summed = summed + parts_ref[source].astype(jnp.float32)
    coupled_ref[...] = jnp.dot(
        mix_ref[...], summed, precision=lax.Precision.HIGHEST, preferred_element_type=jnp.float32
    ).astype(coupled_ref.dtype)


def backward_kernel(slots_ref, earlier_ref, coupled_ref, tiles_ref, out_ref, pairs):
    rows, per_row, proj, tile = tiles_ref.shape
    groups, local, _ = out_ref.shape
    blocks = [earlier_ref[...]] + [coupled_ref[k * proj : (k + 1) * proj] for k in range(BLK)]
    blocks = [b.astype(jnp.float32) for b in blocks]
    for first in range(SLOTS):
        for second in range(SLOTS):
            both = jnp.concatenate([blocks[first], blocks[second]], axis=0)
            pairs[first * SLOTS + second] = both.T.astype(pairs.dtype)

    def row(r, carry):
        at = pl.ds(pl.multiple_of(r * tile, tile), tile)
        values = tiles_ref[r].reshape(per_row * proj, tile)
        chosen = pairs[slots_ref[r, 0] * SLOTS + slots_ref[r, 1]]
        result = jnp.dot(chosen, values, preferred_element_type=jnp.float32)
        out_ref[:, :, at] = result.astype(out_ref.dtype).reshape(groups, local, tile)
        return carry

    lax.fori_loop(0, rows, row, 0, unroll=8)


def from_behind(block, axis, distance):
    devices = range(lax.axis_size(axis))
    route = [(i - distance, i) for i in devices if i - distance in devices]
    return lax.ppermute(block, axis, route)


def mixing(kinds, couplings):
    atoms, width = kinds.shape[0], couplings.shape[1]
    table = jnp.zeros((atoms, width, width), jnp.float32)
    for kind in range(couplings.shape[0]):
        table = table + jnp.where((kinds == kind)[:, None, None], couplings[kind], jnp.float32(0.0))
    same = jnp.eye(atoms, dtype=jnp.bool_)[:, None, :, None]
    spread = jnp.where(same, table[:, :, None, :], jnp.float32(0.0))
    return spread.reshape(atoms * width, atoms * width)


def body(psi, tiles, tile_block, couplings, species):
    splits = lax.axis_size("grid")
    local_bands, slab_points = psi.shape
    rows, per_row, tile, proj = tiles.shape
    bands = local_bands * splits
    points = rows * tile
    flops = 2 * rows * per_row * proj * tile * bands
    moved = 2 * (bands * points + tiles.size)
    slab = lax.axis_index("band")
    slots = tile_block - (slab * BLK - EDGE)
    mix = mixing(species, couplings)
    values = jnp.transpose(tiles, (0, 1, 3, 2))

    spread = lax.all_to_all(
        psi.reshape(local_bands, splits, points), "grid", split_axis=1, concat_axis=0, tiled=True
    ).reshape(splits, local_bands, points)
    own, edge = call(
        forward_kernel,
        (
            jax.ShapeDtypeStruct((BLK * proj, bands), jnp.float32),
            jax.ShapeDtypeStruct((proj, bands), jnp.bfloat16),
        ),
        (pltpu.SMEM, pltpu.VMEM, pltpu.VMEM),
        (pltpu.VMEM, pltpu.VMEM),
        [pltpu.VMEM((SLOTS, proj, bands), jnp.float32)],
        flops,
        moved,
    )(slots, spread, values)
    later = from_behind(edge, "band", -1).astype(jnp.float32)
    last = (BLK - EDGE) * proj
    own = jnp.concatenate([own[:last], own[last:] + later], axis=0).astype(jnp.bfloat16)
    parts = lax.all_to_all(
        jnp.broadcast_to(own[None], (splits,) + own.shape), "grid", 0, 0, tiled=True
    )
    coupled = call(
        couple_kernel,
        jax.ShapeDtypeStruct((BLK * proj, bands), jnp.bfloat16),
        (pltpu.VMEM, pltpu.VMEM),
        pltpu.VMEM,
    )(parts, mix)
    earlier = from_behind(coupled[last:], "band", 1)
    result = call(
        backward_kernel,
        jax.ShapeDtypeStruct((splits, local_bands, points), jnp.bfloat16),
        (pltpu.SMEM, pltpu.VMEM, pltpu.VMEM, pltpu.VMEM),
        pltpu.VMEM,
        [pltpu.VMEM((SLOTS * SLOTS, bands, per_row * proj), jnp.bfloat16)],
        flops,
        moved,
    )(slots, earlier, coupled, values)
    returned = lax.all_to_all(result, "grid", split_axis=0, concat_axis=0, tiled=True)
    return jnp.transpose(returned, (1, 0, 2)).reshape(local_bands, slab_points)


def solution(mesh):
    return jax.shard_map(
        body,
        mesh=mesh,
        in_specs=(
            P("grid", "band"),
            P(("band", "grid"), None, None, None),
            P(("band", "grid"), None),
            P(),
            P("band"),
        ),
        out_specs=P("grid", "band"),
        check_vma=False,
    )
```

```python
import jax
import jax.numpy as jnp
from jax import lax
from jax.experimental import pallas as pl
from jax.experimental.pallas import tpu as pltpu
from jax.sharding import PartitionSpec as P

BLK = 2
EDGE = 1
SLOTS = BLK + EDGE
VMEM_LIMIT = 24 * 1024 * 1024


def whole(space=pltpu.VMEM):
    return pl.BlockSpec(memory_space=space)


def call(kernel, out_shape, in_spaces, out_spaces, scratch=(), flops=0, moved=0):
    single = not isinstance(out_shape, (tuple, list))
    return pl.pallas_call(
        kernel,
        out_shape=out_shape,
        in_specs=[whole(s) for s in in_spaces],
        out_specs=whole(out_spaces) if single else [whole(s) for s in out_spaces],
        scratch_shapes=list(scratch),
        compiler_params=pltpu.CompilerParams(vmem_limit_bytes=VMEM_LIMIT),
        cost_estimate=pl.CostEstimate(flops=flops, bytes_accessed=moved, transcendentals=0),
    )


def slot_of(names_ref, r, j):
    return names_ref[j, r] - (lax.axis_index("band") * BLK - EDGE)


def forward_kernel(names_ref, columns_ref, tiles_ref, own_ref, edge_ref, total):
    rows, per_row, proj, tile = tiles_ref.shape
    groups, local, _ = columns_ref.shape
    bands = groups * local
    total[...] = jnp.zeros_like(total)

    def row(r, carry):
        at = pl.ds(pl.multiple_of(r * tile, tile), tile)
        columns = columns_ref[:, :, at].reshape(bands, tile)
        values = tiles_ref[r].reshape(per_row * proj, tile)
        part = lax.dot_general(
            values, columns, (((1,), (1,)), ((), ())), preferred_element_type=jnp.float32
        )
        for j in range(per_row):
            total[slot_of(names_ref, r, j)] += part[j * proj : (j + 1) * proj]
        return carry

    lax.fori_loop(0, rows, row, 0, unroll=8)
    own_ref[...] = total[EDGE:].reshape(own_ref.shape)
    edge_ref[...] = total[0].astype(edge_ref.dtype)


def share_kernel(own_ref, later_ref, shared_ref):
    last = own_ref.shape[0] - later_ref.shape[0]
    kept = own_ref[:last].astype(shared_ref.dtype)
    summed = (own_ref[last:] + later_ref[...].astype(jnp.float32)).astype(shared_ref.dtype)
    for target in range(shared_ref.shape[0]):
        shared_ref[target, :last] = kept
        shared_ref[target, last:] = summed


def couple_kernel(kinds_ref, parts_ref, couplings_ref, coupled_ref):
    width = couplings_ref.shape[1]
    summed = parts_ref[0].astype(jnp.float32)
    for source in range(1, parts_ref.shape[0]):
        summed = summed + parts_ref[source].astype(jnp.float32)
    for atom in range(kinds_ref.shape[0]):
        at = slice(atom * width, (atom + 1) * width)
        coupled_ref[at] = jnp.dot(
            couplings_ref[kinds_ref[atom]],
            summed[at],
            precision=lax.Precision.HIGHEST,
            preferred_element_type=jnp.float32,
        ).astype(coupled_ref.dtype)


def backward_kernel(names_ref, earlier_ref, coupled_ref, tiles_ref, out_ref, pairs):
    rows, per_row, proj, tile = tiles_ref.shape
    groups, local, _ = out_ref.shape
    blocks = [earlier_ref[...]] + [coupled_ref[k * proj : (k + 1) * proj] for k in range(BLK)]
    blocks = [b.astype(jnp.float32) for b in blocks]
    for first in range(SLOTS):
        for second in range(SLOTS):
            both = jnp.concatenate([blocks[first], blocks[second]], axis=0)
            pairs[first * SLOTS + second] = both.T.astype(pairs.dtype)

    def row(r, carry):
        at = pl.ds(pl.multiple_of(r * tile, tile), tile)
        values = tiles_ref[r].reshape(per_row * proj, tile)
        chosen = pairs[slot_of(names_ref, r, 0) * SLOTS + slot_of(names_ref, r, 1)]
        result = jnp.dot(chosen, values, preferred_element_type=jnp.float32)
        out_ref[:, :, at] = result.astype(out_ref.dtype).reshape(groups, local, tile)
        return carry

    lax.fori_loop(0, rows, row, 0, unroll=8)


def from_behind(block, axis, distance):
    devices = range(lax.axis_size(axis))
    route = [(i - distance, i) for i in devices if i - distance in devices]
    return lax.ppermute(block, axis, route)


def body(psi, tiles, tile_block, couplings, species):
    splits = lax.axis_size("grid")
    local_bands, slab_points = psi.shape
    rows, per_row, tile, proj = tiles.shape
    bands = local_bands * splits
    points = rows * tile
    flops = 2 * rows * per_row * proj * tile * bands
    moved = 2 * (bands * points + tiles.size)
    last = (BLK - EDGE) * proj
    names = tile_block.T
    values = jnp.transpose(tiles, (0, 1, 3, 2))

    spread = lax.all_to_all(
        psi.reshape(local_bands, splits, points), "grid", split_axis=1, concat_axis=0, tiled=True
    ).reshape(splits, local_bands, points)
    own, edge = call(
        forward_kernel,
        (
            jax.ShapeDtypeStruct((BLK * proj, bands), jnp.float32),
            jax.ShapeDtypeStruct((proj, bands), jnp.bfloat16),
        ),
        (pltpu.SMEM, pltpu.VMEM, pltpu.VMEM),
        (pltpu.VMEM, pltpu.VMEM),
        [pltpu.VMEM((SLOTS, proj, bands), jnp.float32)],
        flops,
        moved,
    )(names, spread, values)
    later = from_behind(edge, "band", -1)
    shared = call(
        share_kernel,
        jax.ShapeDtypeStruct((splits,) + own.shape, jnp.bfloat16),
        (pltpu.VMEM, pltpu.VMEM),
        pltpu.VMEM,
    )(own, later)
    parts = lax.all_to_all(shared, "grid", split_axis=0, concat_axis=0, tiled=True)
    coupled = call(
        couple_kernel,
        jax.ShapeDtypeStruct((BLK * proj, bands), jnp.bfloat16),
        (pltpu.SMEM, pltpu.VMEM, pltpu.VMEM),
        pltpu.VMEM,
    )(species, parts, couplings)
    earlier = from_behind(coupled[last:], "band", 1)
    result = call(
        backward_kernel,
        jax.ShapeDtypeStruct((splits, local_bands, points), jnp.bfloat16),
        (pltpu.SMEM, pltpu.VMEM, pltpu.VMEM, pltpu.VMEM),
        pltpu.VMEM,
        [pltpu.VMEM((SLOTS * SLOTS, bands, per_row * proj), jnp.bfloat16)],
        flops,
        moved,
    )(names, earlier, coupled, values)
    returned = lax.all_to_all(result, "grid", split_axis=0, concat_axis=0, tiled=True)
    return jnp.transpose(returned, (1, 0, 2)).reshape(local_bands, slab_points)


def solution(mesh):
    return jax.shard_map(
        body,
        mesh=mesh,
        in_specs=(
            P("grid", "band"),
            P(("band", "grid"), None, None, None),
            P(("band", "grid"), None),
            P(),
            P("band"),
        ),
        out_specs=P("grid", "band"),
        check_vma=False,
    )
```

```python
import jax
import jax.numpy as jnp
from jax import lax
from jax.experimental import pallas as pl
from jax.experimental.pallas import tpu as pltpu
from jax.sharding import PartitionSpec as P

BLK = 2
EDGE = 1
SLOTS = BLK + EDGE
VMEM_LIMIT = 24 * 1024 * 1024


def whole(space=pltpu.VMEM):
    return pl.BlockSpec(memory_space=space)


def call(kernel, out_shape, in_spaces, out_spaces, scratch=(), flops=0, moved=0):
    single = not isinstance(out_shape, (tuple, list))
    return pl.pallas_call(
        kernel,
        out_shape=out_shape,
        in_specs=[whole(s) for s in in_spaces],
        out_specs=whole(out_spaces) if single else [whole(s) for s in out_spaces],
        scratch_shapes=list(scratch),
        compiler_params=pltpu.CompilerParams(vmem_limit_bytes=VMEM_LIMIT),
        cost_estimate=pl.CostEstimate(flops=flops, bytes_accessed=moved, transcendentals=0),
    )


def slot_of(names_ref, r, j):
    return names_ref[j, r] - (lax.axis_index("band") * BLK - EDGE)


def forward_kernel(names_ref, columns_ref, tiles_ref, own_ref, edge_ref, total):
    rows, per_row, proj, tile = tiles_ref.shape
    points = rows * tile
    groups = columns_ref.shape[1] // points
    bands = groups * columns_ref.shape[0]
    depth = per_row * proj
    total[...] = jnp.zeros_like(total)

    def pair(step, carry):
        columns = jnp.concatenate(
            [
                columns_ref[:, pl.ds(pl.multiple_of(g * points + (step * 2 + row) * tile, tile), tile)]
                for row in range(2)
                for g in range(groups)
            ],
            axis=0,
        )
        values = tiles_ref[pl.ds(step * 2, 2)].reshape(2 * depth, tile)
        part = lax.dot_general(
            values, columns, (((1,), (1,)), ((), ())), preferred_element_type=jnp.float32
        )
        for row in range(2):
            for j in range(per_row):
                first = row * depth + j * proj
                total[slot_of(names_ref, step * 2 + row, j)] += part[
                    first : first + proj, row * bands : (row + 1) * bands
                ]
        return carry

    lax.fori_loop(0, rows // 2, pair, 0, unroll=rows // 2)
    own_ref[...] = total[EDGE:].reshape(own_ref.shape)
    edge_ref[...] = total[0].astype(edge_ref.dtype)


def share_kernel(own_ref, later_ref, shared_ref):
    last = own_ref.shape[0] - later_ref.shape[0]
    kept = own_ref[:last].astype(shared_ref.dtype)
    summed = (own_ref[last:] + later_ref[...].astype(jnp.float32)).astype(shared_ref.dtype)
    for target in range(shared_ref.shape[0]):
        shared_ref[target, :last] = kept
        shared_ref[target, last:] = summed


def couple_kernel(kinds_ref, parts_ref, couplings_ref, coupled_ref):
    width = couplings_ref.shape[1]
    summed = parts_ref[0].astype(jnp.float32)
    for source in range(1, parts_ref.shape[0]):
        summed = summed + parts_ref[source].astype(jnp.float32)
    for atom in range(kinds_ref.shape[0]):
        at = slice(atom * width, (atom + 1) * width)
        coupled_ref[at] = jnp.dot(
            couplings_ref[kinds_ref[atom]],
            summed[at],
            precision=lax.Precision.HIGHEST,
            preferred_element_type=jnp.float32,
        ).astype(coupled_ref.dtype)


def backward_kernel(names_ref, earlier_ref, coupled_ref, tiles_ref, out_ref, pairs):
    rows, per_row, proj, tile = tiles_ref.shape
    points = rows * tile
    groups = out_ref.shape[1] // points
    local = out_ref.shape[0]
    blocks = [earlier_ref[...]] + [coupled_ref[k * proj : (k + 1) * proj] for k in range(BLK)]
    blocks = [b.astype(jnp.float32) for b in blocks]
    for first in range(SLOTS):
        for second in range(SLOTS):
            both = jnp.concatenate([blocks[first], blocks[second]], axis=0)
            pairs[first * SLOTS + second] = both.T.astype(pairs.dtype)

    def row(r, carry):
        values = tiles_ref[r].reshape(per_row * proj, tile)
        chosen = pairs[slot_of(names_ref, r, 0) * SLOTS + slot_of(names_ref, r, 1)]
        result = jnp.dot(chosen, values, preferred_element_type=jnp.float32)
        result = result.astype(out_ref.dtype)
        for g in range(groups):
            at = pl.ds(pl.multiple_of(g * points + r * tile, tile), tile)
            out_ref[:, at] = result[g * local : (g + 1) * local]
        return carry

    lax.fori_loop(0, rows, row, 0, unroll=rows)


def from_behind(block, axis, distance):
    devices = range(lax.axis_size(axis))
    route = [(i - distance, i) for i in devices if i - distance in devices]
    return lax.ppermute(block, axis, route)


def body(psi, tiles, tile_block, couplings, species):
    splits = lax.axis_size("grid")
    local_bands = psi.shape[0]
    rows, per_row, tile, proj = tiles.shape
    bands = local_bands * splits
    points = rows * tile
    flops = 2 * rows * per_row * proj * tile * bands
    moved = 2 * (bands * points + tiles.size)
    last = (BLK - EDGE) * proj
    names = tile_block.T
    values = jnp.transpose(tiles, (0, 1, 3, 2))

    spread = lax.all_to_all(psi, "grid", split_axis=1, concat_axis=1, tiled=True)
    own, edge = call(
        forward_kernel,
        (
            jax.ShapeDtypeStruct((BLK * proj, bands), jnp.float32),
            jax.ShapeDtypeStruct((proj, bands), jnp.bfloat16),
        ),
        (pltpu.SMEM, pltpu.VMEM, pltpu.VMEM),
        (pltpu.VMEM, pltpu.VMEM),
        [pltpu.VMEM((SLOTS, proj, bands), jnp.float32)],
        flops,
        moved,
    )(names, spread, values)
    later = from_behind(edge, "band", -1)
    shared = call(
        share_kernel,
        jax.ShapeDtypeStruct((splits,) + own.shape, jnp.bfloat16),
        (pltpu.VMEM, pltpu.VMEM),
        pltpu.VMEM,
    )(own, later)
    parts = lax.all_to_all(shared, "grid", split_axis=0, concat_axis=0, tiled=True)
    coupled = call(
        couple_kernel,
        jax.ShapeDtypeStruct((BLK * proj, bands), jnp.bfloat16),
        (pltpu.SMEM, pltpu.VMEM, pltpu.VMEM),
        pltpu.VMEM,
    )(species, parts, couplings)
    earlier = from_behind(coupled[last:], "band", 1)
    result = call(
        backward_kernel,
        jax.ShapeDtypeStruct(psi.shape, jnp.bfloat16),
        (pltpu.SMEM, pltpu.VMEM, pltpu.VMEM, pltpu.VMEM),
        pltpu.VMEM,
        [pltpu.VMEM((SLOTS * SLOTS, bands, per_row * proj), jnp.bfloat16)],
        flops,
        moved,
    )(names, earlier, coupled, values)
    return lax.all_to_all(result, "grid", split_axis=1, concat_axis=1, tiled=True)


def solution(mesh):
    return jax.shard_map(
        body,
        mesh=mesh,
        in_specs=(
            P("grid", "band"),
            P(("band", "grid"), None, None, None),
            P(("band", "grid"), None),
            P(),
            P("band"),
        ),
        out_specs=P("grid", "band"),
        check_vma=False,
    )
```

```python
import jax
import jax.numpy as jnp
from jax import lax
from jax.experimental import pallas as pl
from jax.experimental.pallas import tpu as pltpu
from jax.sharding import PartitionSpec as P

BLK = 2
EDGE = 1
SLOTS = BLK + EDGE
VMEM_LIMIT = 24 * 1024 * 1024


def whole(space=pltpu.VMEM):
    return pl.BlockSpec(memory_space=space)


def call(kernel, out_shape, in_spaces, out_spaces, scratch=(), flops=0, moved=0):
    single = not isinstance(out_shape, (tuple, list))
    return pl.pallas_call(
        kernel,
        out_shape=out_shape,
        in_specs=[whole(s) for s in in_spaces],
        out_specs=whole(out_spaces) if single else [whole(s) for s in out_spaces],
        scratch_shapes=list(scratch),
        compiler_params=pltpu.CompilerParams(vmem_limit_bytes=VMEM_LIMIT),
        cost_estimate=pl.CostEstimate(flops=flops, bytes_accessed=moved, transcendentals=0),
    )


def slot_of(names_ref, r, j):
    return names_ref[j, r] - (lax.axis_index("band") * BLK - EDGE)


def forward_kernel(names_ref, columns_ref, tiles_ref, own_ref, edge_ref, total):
    rows, per_row, proj, tile = tiles_ref.shape
    points = rows * tile
    groups = columns_ref.shape[1] // points
    bands = groups * columns_ref.shape[0]
    depth = per_row * proj
    total[...] = jnp.zeros_like(total)

    def pair(step, carry):
        columns = jnp.concatenate(
            [
                columns_ref[:, pl.ds(pl.multiple_of(g * points + (step * 2 + row) * tile, tile), tile)]
                for row in range(2)
                for g in range(groups)
            ],
            axis=0,
        )
        values = tiles_ref[pl.ds(step * 2, 2)].reshape(2 * depth, tile)
        part = lax.dot_general(
            values, columns, (((1,), (1,)), ((), ())), preferred_element_type=jnp.float32
        )
        for row in range(2):
            for j in range(per_row):
                first = row * depth + j * proj
                total[slot_of(names_ref, step * 2 + row, j)] += part[
                    first : first + proj, row * bands : (row + 1) * bands
                ]
        return carry

    lax.fori_loop(0, rows // 2, pair, 0, unroll=rows // 2)
    own_ref[...] = total[EDGE:].reshape(own_ref.shape)
    edge_ref[...] = total[0].astype(edge_ref.dtype)


def share_kernel(own_ref, later_ref, shared_ref):
    last = own_ref.shape[0] - later_ref.shape[0]
    kept = own_ref[:last].astype(shared_ref.dtype)
    summed = (own_ref[last:] + later_ref[...].astype(jnp.float32)).astype(shared_ref.dtype)
    for target in range(shared_ref.shape[0]):
        shared_ref[target, :last] = kept
        shared_ref[target, last:] = summed


def couple_kernel(kinds_ref, parts_ref, couplings_ref, coupled_ref):
    width = couplings_ref.shape[1]
    summed = parts_ref[0].astype(jnp.float32)
    for source in range(1, parts_ref.shape[0]):
        summed = summed + parts_ref[source].astype(jnp.float32)
    for atom in range(kinds_ref.shape[0]):
        at = slice(atom * width, (atom + 1) * width)
        coupled_ref[at] = jnp.dot(
            couplings_ref[kinds_ref[atom]],
            summed[at],
            precision=lax.Precision.HIGHEST,
            preferred_element_type=jnp.float32,
        ).astype(coupled_ref.dtype)


def backward_kernel(names_ref, earlier_ref, coupled_ref, tiles_ref, out_ref, pairs):
    rows, per_row, proj, tile = tiles_ref.shape
    points = rows * tile
    groups = out_ref.shape[1] // points
    local = out_ref.shape[0]
    blocks = [earlier_ref[...]] + [coupled_ref[k * proj : (k + 1) * proj] for k in range(BLK)]
    blocks = [b.astype(jnp.float32) for b in blocks]
    for first in range(SLOTS):
        for second in range(SLOTS):
            both = jnp.concatenate([blocks[first], blocks[second]], axis=0)
            pairs[first * SLOTS + second] = both.T.astype(pairs.dtype)

    def row(r, carry):
        values = tiles_ref[r].reshape(per_row * proj, tile)
        chosen = pairs[slot_of(names_ref, r, 0) * SLOTS + slot_of(names_ref, r, 1)]
        result = jnp.dot(chosen, values, preferred_element_type=jnp.float32)
        result = result.astype(out_ref.dtype)
        for g in range(groups):
            at = pl.ds(pl.multiple_of(g * points + r * tile, tile), tile)
            out_ref[:, at] = result[g * local : (g + 1) * local]
        return carry

    lax.fori_loop(0, rows, row, 0, unroll=rows)


def from_behind(block, axis, distance):
    size = lax.axis_size(axis)
    return lax.ppermute(block, axis, [(i, (i + distance) % size) for i in range(size)])


def body(psi, tiles, tile_block, couplings, species):
    splits = lax.axis_size("grid")
    local_bands = psi.shape[0]
    rows, per_row, tile, proj = tiles.shape
    bands = local_bands * splits
    points = rows * tile
    flops = 2 * rows * per_row * proj * tile * bands
    moved = 2 * (bands * points + tiles.size)
    last = (BLK - EDGE) * proj
    names = tile_block.T
    values = jnp.transpose(tiles, (0, 1, 3, 2))

    spread = lax.all_to_all(psi, "grid", split_axis=1, concat_axis=1, tiled=True)
    own, edge = call(
        forward_kernel,
        (
            jax.ShapeDtypeStruct((BLK * proj, bands), jnp.float32),
            jax.ShapeDtypeStruct((proj, bands), jnp.bfloat16),
        ),
        (pltpu.SMEM, pltpu.VMEM, pltpu.VMEM),
        (pltpu.VMEM, pltpu.VMEM),
        [pltpu.VMEM((SLOTS, proj, bands), jnp.float32)],
        flops,
        moved,
    )(names, spread, values)
    later = from_behind(edge, "band", -1)
    shared = call(
        share_kernel,
        jax.ShapeDtypeStruct((splits,) + own.shape, jnp.bfloat16),
        (pltpu.VMEM, pltpu.VMEM),
        pltpu.VMEM,
    )(own, later)
    parts = lax.all_to_all(shared, "grid", split_axis=0, concat_axis=0, tiled=True)
    coupled = call(
        couple_kernel,
        jax.ShapeDtypeStruct((BLK * proj, bands), jnp.bfloat16),
        (pltpu.SMEM, pltpu.VMEM, pltpu.VMEM),
        pltpu.VMEM,
    )(species, parts, couplings)
    earlier = from_behind(coupled[last:], "band", 1)
    result = call(
        backward_kernel,
        jax.ShapeDtypeStruct(psi.shape, jnp.bfloat16),
        (pltpu.SMEM, pltpu.VMEM, pltpu.VMEM, pltpu.VMEM),
        pltpu.VMEM,
        [pltpu.VMEM((SLOTS * SLOTS, bands, per_row * proj), jnp.bfloat16)],
        flops,
        moved,
    )(names, earlier, coupled, values)
    return lax.all_to_all(result, "grid", split_axis=1, concat_axis=1, tiled=True)


def solution(mesh):
    return jax.shard_map(
        body,
        mesh=mesh,
        in_specs=(
            P("grid", "band"),
            P(("band", "grid"), None, None, None),
            P(("band", "grid"), None),
            P(),
            P("band"),
        ),
        out_specs=P("grid", "band"),
        check_vma=False,
    )
```

```python
import jax
import jax.numpy as jnp
from jax import lax
from jax.experimental import pallas as pl
from jax.experimental.pallas import tpu as pltpu
from jax.sharding import PartitionSpec as P

BLK = 2
EDGE = 1
SLOTS = BLK + EDGE
AHEAD = 8
VMEM_LIMIT = 24 * 1024 * 1024


def whole(space=pltpu.VMEM):
    return pl.BlockSpec(memory_space=space)


def call(kernel, out_shape, in_spaces, out_spaces, scratch=(), flops=0, moved=0):
    single = not isinstance(out_shape, (tuple, list))
    return pl.pallas_call(
        kernel,
        out_shape=out_shape,
        in_specs=[whole(s) for s in in_spaces],
        out_specs=whole(out_spaces) if single else [whole(s) for s in out_spaces],
        scratch_shapes=list(scratch),
        compiler_params=pltpu.CompilerParams(vmem_limit_bytes=VMEM_LIMIT),
        cost_estimate=pl.CostEstimate(flops=flops, bytes_accessed=moved, transcendentals=0),
    )


def slot_of(names_ref, r, j):
    return names_ref[j, r] - (lax.axis_index("band") * BLK - EDGE)


def forward_kernel(
    names_any,
    kinds_any,
    columns_ref,
    tiles_ref,
    couplings_ref,
    own_ref,
    edge_ref,
    matrices_ref,
    total,
    early,
    names_ref,
    kinds_ref,
    sems,
):
    copies = [
        pltpu.make_async_copy(names_any, names_ref, sems.at[0]),
        pltpu.make_async_copy(kinds_any, kinds_ref, sems.at[1]),
    ]
    for copy in copies:
        copy.start()
    rows, per_row, proj, tile = tiles_ref.shape
    points = rows * tile
    groups = columns_ref.shape[1] // points
    bands = groups * columns_ref.shape[0]
    depth = per_row * proj
    total[...] = jnp.zeros_like(total)

    def products(step):
        columns = jnp.concatenate(
            [
                columns_ref[:, pl.ds(pl.multiple_of(g * points + (step * 2 + row) * tile, tile), tile)]
                for row in range(2)
                for g in range(groups)
            ],
            axis=0,
        )
        values = tiles_ref[pl.ds(step * 2, 2)].reshape(2 * depth, tile)
        part = lax.dot_general(
            values, columns, (((1,), (1,)), ((), ())), preferred_element_type=jnp.float32
        )
        return part[:depth, :bands], part[depth:, bands:]

    def add(r, part):
        for j in range(per_row):
            total[slot_of(names_ref, r, j)] += part[j * proj : (j + 1) * proj]

    def pair(step, carry):
        for row, part in enumerate(products(step)):
            add(step * 2 + row, part)
        return carry

    ahead = early.shape[0] // 2
    for step in range(ahead):
        for row, part in enumerate(products(step)):
            early[step * 2 + row] = part
    for copy in copies:
        copy.wait()
    for r in range(2 * ahead):
        add(r, early[r])
    lax.fori_loop(ahead, rows // 2, pair, 0, unroll=rows // 2 - ahead)
    own_ref[...] = total[EDGE:].reshape(own_ref.shape)
    edge_ref[...] = total[0].astype(edge_ref.dtype)
    for atom in range(kinds_ref.shape[0]):
        matrices_ref[atom] = couplings_ref[kinds_ref[atom]]


def share_kernel(own_ref, later_ref, shared_ref):
    last = own_ref.shape[0] - later_ref.shape[0]
    kept = own_ref[:last].astype(shared_ref.dtype)
    summed = (own_ref[last:] + later_ref[...].astype(jnp.float32)).astype(shared_ref.dtype)
    for target in range(shared_ref.shape[0]):
        shared_ref[target, :last] = kept
        shared_ref[target, last:] = summed


def couple_kernel(parts_ref, matrices_ref, coupled_ref):
    atoms, width, _ = matrices_ref.shape
    summed = parts_ref[0].astype(jnp.float32)
    for source in range(1, parts_ref.shape[0]):
        summed = summed + parts_ref[source].astype(jnp.float32)
    for atom in range(atoms):
        at = slice(atom * width, (atom + 1) * width)
        coupled_ref[at] = jnp.dot(
            matrices_ref[atom],
            summed[at],
            precision=lax.Precision.HIGHEST,
            preferred_element_type=jnp.float32,
        ).astype(coupled_ref.dtype)


def backward_kernel(
    names_any, earlier_ref, coupled_ref, tiles_ref, out_ref, pairs, names_ref, sem
):
    copy = pltpu.make_async_copy(names_any, names_ref, sem)
    copy.start()
    rows, per_row, proj, tile = tiles_ref.shape
    points = rows * tile
    groups = out_ref.shape[1] // points
    local = out_ref.shape[0]
    blocks = [earlier_ref[...]] + [coupled_ref[k * proj : (k + 1) * proj] for k in range(BLK)]
    blocks = [b.astype(jnp.float32) for b in blocks]
    for first in range(SLOTS):
        for second in range(SLOTS):
            both = jnp.concatenate([blocks[first], blocks[second]], axis=0)
            pairs[first * SLOTS + second] = both.T.astype(pairs.dtype)
    copy.wait()

    def row(r, carry):
        values = tiles_ref[r].reshape(per_row * proj, tile)
        chosen = pairs[slot_of(names_ref, r, 0) * SLOTS + slot_of(names_ref, r, 1)]
        result = jnp.dot(chosen, values, preferred_element_type=jnp.float32)
        result = result.astype(out_ref.dtype)
        for g in range(groups):
            at = pl.ds(pl.multiple_of(g * points + r * tile, tile), tile)
            out_ref[:, at] = result[g * local : (g + 1) * local]
        return carry

    lax.fori_loop(0, rows, row, 0, unroll=rows)


def from_behind(block, axis, distance):
    size = lax.axis_size(axis)
    return lax.ppermute(block, axis, [(i, (i + distance) % size) for i in range(size)])


def body(psi, tiles, tile_block, couplings, species):
    splits = lax.axis_size("grid")
    local_bands = psi.shape[0]
    rows, per_row, tile, proj = tiles.shape
    bands = local_bands * splits
    points = rows * tile
    flops = 2 * rows * per_row * proj * tile * bands
    moved = 2 * (bands * points + tiles.size)
    last = (BLK - EDGE) * proj
    names = tile_block.T
    values = jnp.transpose(tiles, (0, 1, 3, 2))

    spread = lax.all_to_all(psi, "grid", split_axis=1, concat_axis=1, tiled=True)
    own, edge, matrices = call(
        forward_kernel,
        (
            jax.ShapeDtypeStruct((BLK * proj, bands), jnp.float32),
            jax.ShapeDtypeStruct((proj, bands), jnp.bfloat16),
            jax.ShapeDtypeStruct(species.shape + couplings.shape[1:], jnp.float32),
        ),
        (pl.ANY, pl.ANY, pltpu.VMEM, pltpu.VMEM, pltpu.VMEM),
        (pltpu.VMEM, pltpu.VMEM, pltpu.VMEM),
        [
            pltpu.VMEM((SLOTS, proj, bands), jnp.float32),
            pltpu.VMEM((2 * AHEAD, per_row * proj, bands), jnp.float32),
            pltpu.SMEM(names.shape, jnp.int32),
            pltpu.SMEM(species.shape, jnp.int32),
            pltpu.SemaphoreType.DMA((2,)),
        ],
        flops,
        moved,
    )(names, species, spread, values, couplings)
    later = from_behind(edge, "band", -1)
    shared = call(
        share_kernel,
        jax.ShapeDtypeStruct((splits,) + own.shape, jnp.bfloat16),
        (pltpu.VMEM, pltpu.VMEM),
        pltpu.VMEM,
    )(own, later)
    parts = lax.all_to_all(shared, "grid", split_axis=0, concat_axis=0, tiled=True)
    coupled = call(
        couple_kernel,
        jax.ShapeDtypeStruct((BLK * proj, bands), jnp.bfloat16),
        (pltpu.VMEM, pltpu.VMEM),
        pltpu.VMEM,
    )(parts, matrices)
    earlier = from_behind(coupled[last:], "band", 1)
    result = call(
        backward_kernel,
        jax.ShapeDtypeStruct(psi.shape, jnp.bfloat16),
        (pl.ANY, pltpu.VMEM, pltpu.VMEM, pltpu.VMEM),
        pltpu.VMEM,
        [
            pltpu.VMEM((SLOTS * SLOTS, bands, per_row * proj), jnp.bfloat16),
            pltpu.SMEM(names.shape, jnp.int32),
            pltpu.SemaphoreType.DMA(()),
        ],
        flops,
        moved,
    )(names, earlier, coupled, values)
    return lax.all_to_all(result, "grid", split_axis=1, concat_axis=1, tiled=True)


def solution(mesh):
    return jax.shard_map(
        body,
        mesh=mesh,
        in_specs=(
            P("grid", "band"),
            P(("band", "grid"), None, None, None),
            P(("band", "grid"), None),
            P(),
            P("band"),
        ),
        out_specs=P("grid", "band"),
        check_vma=False,
    )
```

```python
import functools

import jax
import jax.numpy as jnp
from jax import lax
from jax.experimental import pallas as pl
from jax.experimental.pallas import tpu as pltpu
from jax.sharding import PartitionSpec as P

BLK = 2
EDGE = 1
SLOTS = BLK + EDGE
AHEAD = 8
VMEM_LIMIT = 24 * 1024 * 1024


def whole(space=pltpu.VMEM):
    return pl.BlockSpec(memory_space=space)


def call(kernel, out_shape, in_spaces, out_spaces, scratch=(), flops=0, moved=0):
    single = not isinstance(out_shape, (tuple, list))
    return pl.pallas_call(
        kernel,
        out_shape=out_shape,
        in_specs=[whole(s) for s in in_spaces],
        out_specs=whole(out_spaces) if single else [whole(s) for s in out_spaces],
        scratch_shapes=list(scratch),
        compiler_params=pltpu.CompilerParams(vmem_limit_bytes=VMEM_LIMIT),
        cost_estimate=pl.CostEstimate(flops=flops, bytes_accessed=moved, transcendentals=0),
    )


def slot_of(names_ref, r, j):
    return names_ref[j, r] - (lax.axis_index("band") * BLK - EDGE)


def forward_kernel(
    names_any,
    kinds_any,
    columns_ref,
    tiles_ref,
    couplings_ref,
    own_ref,
    edge_ref,
    matrices_ref,
    total,
    early,
    names_ref,
    kinds_ref,
    sems,
):
    copies = [
        pltpu.make_async_copy(names_any, names_ref, sems.at[0]),
        pltpu.make_async_copy(kinds_any, kinds_ref, sems.at[1]),
    ]
    for copy in copies:
        copy.start()
    rows, per_row, proj, tile = tiles_ref.shape
    points = rows * tile
    groups = columns_ref.shape[1] // points
    bands = groups * columns_ref.shape[0]
    depth = per_row * proj
    total[...] = jnp.zeros_like(total)

    def products(step):
        columns = jnp.concatenate(
            [
                columns_ref[:, pl.ds(pl.multiple_of(g * points + (step * 2 + row) * tile, tile), tile)]
                for row in range(2)
                for g in range(groups)
            ],
            axis=0,
        )
        values = tiles_ref[pl.ds(step * 2, 2)].reshape(2 * depth, tile)
        part = lax.dot_general(
            values, columns, (((1,), (1,)), ((), ())), preferred_element_type=jnp.float32
        )
        return part[:depth, :bands], part[depth:, bands:]

    def add(r, part):
        for j in range(per_row):
            total[slot_of(names_ref, r, j)] += part[j * proj : (j + 1) * proj]

    def pair(step, carry):
        for row, part in enumerate(products(step)):
            add(step * 2 + row, part)
        return carry

    ahead = early.shape[0] // 2
    for step in range(ahead):
        for row, part in enumerate(products(step)):
            early[step * 2 + row] = part
    for copy in copies:
        copy.wait()
    for r in range(2 * ahead):
        add(r, early[r])
    lax.fori_loop(ahead, rows // 2, pair, 0, unroll=rows // 2 - ahead)
    own_ref[...] = total[EDGE:].reshape(own_ref.shape)
    edge_ref[...] = total[0].astype(edge_ref.dtype)
    for atom in range(kinds_ref.shape[0]):
        matrices_ref[atom] = couplings_ref[kinds_ref[atom]]


def share_kernel(own_ref, later_ref, shared_ref):
    last = own_ref.shape[0] - later_ref.shape[0]
    kept = own_ref[:last].astype(shared_ref.dtype)
    summed = (own_ref[last:] + later_ref[...].astype(jnp.float32)).astype(shared_ref.dtype)
    for target in range(shared_ref.shape[0]):
        shared_ref[target, :last] = kept
        shared_ref[target, last:] = summed


def couple_kernel(parts_ref, matrices_ref, coupled_ref):
    atoms, width, _ = matrices_ref.shape
    summed = parts_ref[0].astype(jnp.float32)
    for source in range(1, parts_ref.shape[0]):
        summed = summed + parts_ref[source].astype(jnp.float32)
    for atom in range(atoms):
        at = slice(atom * width, (atom + 1) * width)
        coupled_ref[at] = jnp.dot(
            matrices_ref[atom],
            summed[at],
            precision=lax.Precision.HIGHEST,
            preferred_element_type=jnp.float32,
        ).astype(coupled_ref.dtype)


def backward_kernel(
    order, names_any, earlier_ref, coupled_ref, tiles_ref, out_ref, pairs, names_ref, sem
):
    copy = pltpu.make_async_copy(names_any, names_ref, sem)
    copy.start()
    rows, per_row, proj, tile = tiles_ref.shape
    points = rows * tile
    groups = out_ref.shape[1] // points
    local = out_ref.shape[0]
    blocks = [earlier_ref[...]] + [coupled_ref[k * proj : (k + 1) * proj] for k in range(BLK)]
    blocks = [b.astype(jnp.float32) for b in blocks]
    for first in range(SLOTS):
        for second in range(SLOTS):
            both = jnp.concatenate([blocks[first], blocks[second]], axis=0)
            pairs[first * SLOTS + second] = both.T.astype(pairs.dtype)
    copy.wait()

    def row(r, carry):
        values = tiles_ref[r].reshape(per_row * proj, tile)
        chosen = pairs[slot_of(names_ref, r, 0) * SLOTS + slot_of(names_ref, r, 1)]
        result = jnp.dot(chosen, values, preferred_element_type=jnp.float32)
        result = result.astype(out_ref.dtype)
        for g in range(groups):
            at = pl.ds(pl.multiple_of(order.index(g) * points + r * tile, tile), tile)
            out_ref[:, at] = result[g * local : (g + 1) * local]
        return carry

    lax.fori_loop(0, rows, row, 0, unroll=rows)


def place_kernel(order, blocks_ref, out_any, sems):
    width = blocks_ref.shape[1] // len(order)
    copies = [
        pltpu.make_async_copy(
            blocks_ref.at[:, pl.ds(k * width, width)],
            out_any.at[:, pl.ds(device * width, width)],
            sems.at[k],
        )
        for k, device in enumerate(order)
    ]
    for copy in copies:
        copy.start()
    for copy in copies:
        copy.wait()


def from_behind(block, axis, distance):
    size = lax.axis_size(axis)
    return lax.ppermute(block, axis, [(i, (i + distance) % size) for i in range(size)])


def body(psi, tiles, tile_block, couplings, species):
    splits = lax.axis_size("grid")
    local_bands = psi.shape[0]
    rows, per_row, tile, proj = tiles.shape
    bands = local_bands * splits
    points = rows * tile
    flops = 2 * rows * per_row * proj * tile * bands
    moved = 2 * (bands * points + tiles.size)
    last = (BLK - EDGE) * proj
    names = tile_block.T
    order = [i ^ (i >> 1) for i in range(splits)]
    values = jnp.transpose(tiles, (0, 1, 3, 2))

    spread = lax.all_to_all(psi, "grid", split_axis=1, concat_axis=1, tiled=True)
    own, edge, matrices = call(
        forward_kernel,
        (
            jax.ShapeDtypeStruct((BLK * proj, bands), jnp.float32),
            jax.ShapeDtypeStruct((proj, bands), jnp.bfloat16),
            jax.ShapeDtypeStruct(species.shape + couplings.shape[1:], jnp.float32),
        ),
        (pl.ANY, pl.ANY, pltpu.VMEM, pltpu.VMEM, pltpu.VMEM),
        (pltpu.VMEM, pltpu.VMEM, pltpu.VMEM),
        [
            pltpu.VMEM((SLOTS, proj, bands), jnp.float32),
            pltpu.VMEM((2 * AHEAD, per_row * proj, bands), jnp.float32),
            pltpu.SMEM(names.shape, jnp.int32),
            pltpu.SMEM(species.shape, jnp.int32),
            pltpu.SemaphoreType.DMA((2,)),
        ],
        flops,
        moved,
    )(names, species, spread, values, couplings)
    later = from_behind(edge, "band", -1)
    shared = call(
        share_kernel,
        jax.ShapeDtypeStruct((splits,) + own.shape, jnp.bfloat16),
        (pltpu.VMEM, pltpu.VMEM),
        pltpu.VMEM,
    )(own, later)
    parts = lax.all_to_all(shared, "grid", split_axis=0, concat_axis=0, tiled=True)
    coupled = call(
        couple_kernel,
        jax.ShapeDtypeStruct((BLK * proj, bands), jnp.bfloat16),
        (pltpu.VMEM, pltpu.VMEM),
        pltpu.VMEM,
    )(parts, matrices)
    earlier = from_behind(coupled[last:], "band", 1)
    result = call(
        functools.partial(backward_kernel, order),
        jax.ShapeDtypeStruct(psi.shape, jnp.bfloat16),
        (pl.ANY, pltpu.VMEM, pltpu.VMEM, pltpu.VMEM),
        pltpu.VMEM,
        [
            pltpu.VMEM((SLOTS * SLOTS, bands, per_row * proj), jnp.bfloat16),
            pltpu.SMEM(names.shape, jnp.int32),
            pltpu.SemaphoreType.DMA(()),
        ],
        flops,
        moved,
    )(names, earlier, coupled, values)
    returned = lax.all_to_all(
        result, "grid", split_axis=1, concat_axis=1, tiled=True, axis_index_groups=[order]
    )
    return call(
        functools.partial(place_kernel, order),
        jax.ShapeDtypeStruct(psi.shape, jnp.bfloat16),
        (pltpu.VMEM,),
        pl.ANY,
        [pltpu.SemaphoreType.DMA((splits,))],
    )(returned)


def solution(mesh):
    return jax.shard_map(
        body,
        mesh=mesh,
        in_specs=(
            P("grid", "band"),
            P(("band", "grid"), None, None, None),
            P(("band", "grid"), None),
            P(),
            P("band"),
        ),
        out_specs=P("grid", "band"),
        check_vma=False,
    )
```

```python
import functools

import jax
import jax.numpy as jnp
from jax import lax
from jax.experimental import pallas as pl
from jax.experimental.pallas import tpu as pltpu
from jax.sharding import PartitionSpec as P

BLK = 2
EDGE = 1
SLOTS = BLK + EDGE
AHEAD = 16
VMEM_LIMIT = 24 * 1024 * 1024


def whole(space=pltpu.VMEM):
    return pl.BlockSpec(memory_space=space)


def call(kernel, out_shape, in_spaces, out_spaces, scratch=(), flops=0, moved=0):
    single = not isinstance(out_shape, (tuple, list))
    return pl.pallas_call(
        kernel,
        out_shape=out_shape,
        in_specs=[whole(s) for s in in_spaces],
        out_specs=whole(out_spaces) if single else [whole(s) for s in out_spaces],
        scratch_shapes=list(scratch),
        compiler_params=pltpu.CompilerParams(vmem_limit_bytes=VMEM_LIMIT),
        cost_estimate=pl.CostEstimate(flops=flops, bytes_accessed=moved, transcendentals=0),
    )


def slot_of(names_ref, r, j):
    return names_ref[j, r] - (lax.axis_index("band") * BLK - EDGE)


def forward_kernel(
    names_any,
    kinds_any,
    columns_ref,
    tiles_ref,
    couplings_ref,
    own_ref,
    edge_ref,
    matrices_ref,
    total,
    early,
    names_ref,
    kinds_ref,
    sems,
):
    copies = [
        pltpu.make_async_copy(names_any, names_ref, sems.at[0]),
        pltpu.make_async_copy(kinds_any, kinds_ref, sems.at[1]),
    ]
    for copy in copies:
        copy.start()
    rows, per_row, proj, tile = tiles_ref.shape
    points = rows * tile
    groups = columns_ref.shape[1] // points
    bands = groups * columns_ref.shape[0]
    depth = per_row * proj
    total[...] = jnp.zeros_like(total)

    def products(step):
        columns = jnp.concatenate(
            [
                columns_ref[:, pl.ds(pl.multiple_of(g * points + (step * 2 + row) * tile, tile), tile)]
                for row in range(2)
                for g in range(groups)
            ],
            axis=0,
        )
        values = tiles_ref[pl.ds(step * 2, 2)].reshape(2 * depth, tile)
        part = lax.dot_general(
            values, columns, (((1,), (1,)), ((), ())), preferred_element_type=jnp.float32
        )
        return part[:depth, :bands], part[depth:, bands:]

    def add(r, part):
        for j in range(per_row):
            total[slot_of(names_ref, r, j)] += part[j * proj : (j + 1) * proj]

    def pair(step, carry):
        for row, part in enumerate(products(step)):
            add(step * 2 + row, part)
        return carry

    ahead = early.shape[0] // 2
    for step in range(ahead):
        for row, part in enumerate(products(step)):
            early[step * 2 + row] = part
    for copy in copies:
        copy.wait()
    for r in range(2 * ahead):
        add(r, early[r])
    lax.fori_loop(ahead, rows // 2, pair, 0, unroll=rows // 2 - ahead)
    own_ref[...] = total[EDGE:].reshape(own_ref.shape)
    edge_ref[...] = total[0].astype(edge_ref.dtype)
    for atom in range(kinds_ref.shape[0]):
        matrices_ref[atom] = couplings_ref[kinds_ref[atom]]


def share_kernel(own_ref, later_ref, shared_ref):
    last = own_ref.shape[0] - later_ref.shape[0]
    kept = own_ref[:last].astype(shared_ref.dtype)
    summed = (own_ref[last:] + later_ref[...].astype(jnp.float32)).astype(shared_ref.dtype)
    for target in range(shared_ref.shape[0]):
        shared_ref[target, :last] = kept
        shared_ref[target, last:] = summed


def couple_kernel(parts_ref, matrices_ref, coupled_ref):
    atoms, width, _ = matrices_ref.shape
    summed = parts_ref[0].astype(jnp.float32)
    for source in range(1, parts_ref.shape[0]):
        summed = summed + parts_ref[source].astype(jnp.float32)
    for atom in range(atoms):
        at = slice(atom * width, (atom + 1) * width)
        coupled_ref[at] = jnp.dot(
            matrices_ref[atom],
            summed[at],
            precision=lax.Precision.HIGHEST,
            preferred_element_type=jnp.float32,
        ).astype(coupled_ref.dtype)


def backward_kernel(
    order, names_any, earlier_ref, coupled_ref, tiles_ref, out_ref, pairs, names_ref, sem
):
    copy = pltpu.make_async_copy(names_any, names_ref, sem)
    copy.start()
    rows, per_row, proj, tile = tiles_ref.shape
    points = rows * tile
    groups = out_ref.shape[1] // points
    local = out_ref.shape[0]
    blocks = [earlier_ref[...]] + [coupled_ref[k * proj : (k + 1) * proj] for k in range(BLK)]
    blocks = [b.astype(jnp.float32) for b in blocks]
    blocks = [jnp.concatenate([b, b], axis=0).T for b in blocks]
    left = lax.broadcasted_iota(jnp.int32, blocks[0].shape, 1) < proj
    for first in range(SLOTS):
        for second in range(SLOTS):
            both = jnp.where(left, blocks[first], blocks[second])
            pairs[first * SLOTS + second] = both.astype(pairs.dtype)
    copy.wait()

    def row(r, carry):
        values = tiles_ref[r].reshape(per_row * proj, tile)
        chosen = pairs[slot_of(names_ref, r, 0) * SLOTS + slot_of(names_ref, r, 1)]
        result = jnp.dot(chosen, values, preferred_element_type=jnp.float32)
        result = result.astype(out_ref.dtype)
        for g in range(groups):
            at = pl.ds(pl.multiple_of(order.index(g) * points + r * tile, tile), tile)
            out_ref[:, at] = result[g * local : (g + 1) * local]
        return carry

    lax.fori_loop(0, rows, row, 0, unroll=rows)


def from_behind(block, axis, distance):
    size = lax.axis_size(axis)
    return lax.ppermute(block, axis, [(i, (i + distance) % size) for i in range(size)])


def place_kernel(order, blocks_ref, out_any, sems):
    width = blocks_ref.shape[1] // len(order)
    copies = [
        pltpu.make_async_copy(
            blocks_ref.at[:, pl.ds(k * width, width)],
            out_any.at[:, pl.ds(device * width, width)],
            sems.at[k],
        )
        for k, device in enumerate(order)
    ]
    for copy in copies:
        copy.start()
    for copy in copies:
        copy.wait()


def body(psi, tiles, tile_block, couplings, species):
    splits = lax.axis_size("grid")
    local_bands = psi.shape[0]
    rows, per_row, tile, proj = tiles.shape
    bands = local_bands * splits
    points = rows * tile
    flops = 2 * rows * per_row * proj * tile * bands
    moved = 2 * (bands * points + tiles.size)
    last = (BLK - EDGE) * proj
    names = tile_block.T
    order = [i ^ (i >> 1) for i in range(splits)]
    order = order[splits // 2 :] + order[: splits // 2]
    values = jnp.transpose(tiles, (0, 1, 3, 2))

    spread = lax.all_to_all(psi, "grid", split_axis=1, concat_axis=1, tiled=True)
    own, edge, matrices = call(
        forward_kernel,
        (
            jax.ShapeDtypeStruct((BLK * proj, bands), jnp.float32),
            jax.ShapeDtypeStruct((proj, bands), jnp.bfloat16),
            jax.ShapeDtypeStruct(species.shape + couplings.shape[1:], jnp.float32),
        ),
        (pl.ANY, pl.ANY, pltpu.VMEM, pltpu.VMEM, pltpu.VMEM),
        (pltpu.VMEM, pltpu.VMEM, pltpu.VMEM),
        [
            pltpu.VMEM((SLOTS, proj, bands), jnp.float32),
            pltpu.VMEM((2 * AHEAD, per_row * proj, bands), jnp.float32),
            pltpu.SMEM(names.shape, jnp.int32),
            pltpu.SMEM(species.shape, jnp.int32),
            pltpu.SemaphoreType.DMA((2,)),
        ],
        flops,
        moved,
    )(names, species, spread, values, couplings)
    later = from_behind(edge, "band", -1)
    shared = call(
        share_kernel,
        jax.ShapeDtypeStruct((splits,) + own.shape, jnp.bfloat16),
        (pltpu.VMEM, pltpu.VMEM),
        pltpu.VMEM,
    )(own, later)
    parts = lax.all_to_all(shared, "grid", split_axis=0, concat_axis=0, tiled=True)
    coupled = call(
        couple_kernel,
        jax.ShapeDtypeStruct((BLK * proj, bands), jnp.bfloat16),
        (pltpu.VMEM, pltpu.VMEM),
        pltpu.VMEM,
    )(parts, matrices)
    earlier = from_behind(coupled[last:], "band", 1)
    result = call(
        functools.partial(backward_kernel, order),
        jax.ShapeDtypeStruct(psi.shape, jnp.bfloat16),
        (pl.ANY, pltpu.VMEM, pltpu.VMEM, pltpu.VMEM),
        pltpu.VMEM,
        [
            pltpu.VMEM((SLOTS * SLOTS, bands, per_row * proj), jnp.bfloat16),
            pltpu.SMEM(names.shape, jnp.int32),
            pltpu.SemaphoreType.DMA(()),
        ],
        flops,
        moved,
    )(names, earlier, coupled, values)
    returned = lax.all_to_all(
        result, "grid", split_axis=1, concat_axis=1, tiled=True, axis_index_groups=[order]
    )
    return call(
        functools.partial(place_kernel, order),
        jax.ShapeDtypeStruct(psi.shape, jnp.bfloat16),
        (pltpu.VMEM,),
        pl.ANY,
        [pltpu.SemaphoreType.DMA((splits,))],
    )(returned)


def solution(mesh):
    return jax.shard_map(
        body,
        mesh=mesh,
        in_specs=(
            P("grid", "band"),
            P(("band", "grid"), None, None, None),
            P(("band", "grid"), None),
            P(),
            P("band"),
        ),
        out_specs=P("grid", "band"),
        check_vma=False,
    )
```

```python
import functools

import jax
import jax.numpy as jnp
from jax import lax
from jax.experimental import pallas as pl
from jax.experimental.pallas import tpu as pltpu
from jax.sharding import PartitionSpec as P

BLK = 2
EDGE = 1
SLOTS = BLK + EDGE
AHEAD = 8
VMEM_LIMIT = 24 * 1024 * 1024


def whole(space=pltpu.VMEM):
    return pl.BlockSpec(memory_space=space)


def call(kernel, out_shape, in_spaces, out_spaces, scratch=(), flops=0, moved=0):
    single = not isinstance(out_shape, (tuple, list))
    return pl.pallas_call(
        kernel,
        out_shape=out_shape,
        in_specs=[whole(s) for s in in_spaces],
        out_specs=whole(out_spaces) if single else [whole(s) for s in out_spaces],
        scratch_shapes=list(scratch),
        compiler_params=pltpu.CompilerParams(vmem_limit_bytes=VMEM_LIMIT),
        cost_estimate=pl.CostEstimate(flops=flops, bytes_accessed=moved, transcendentals=0),
    )


def slot_of(names_ref, r, j):
    return names_ref[j, r] - (lax.axis_index("band") * BLK - EDGE)


def forward_kernel(
    names_any,
    kinds_any,
    columns_ref,
    tiles_ref,
    couplings_ref,
    own_ref,
    edge_ref,
    matrices_ref,
    total,
    early,
    names_ref,
    kinds_ref,
    sems,
):
    copies = [
        pltpu.make_async_copy(names_any, names_ref, sems.at[0]),
        pltpu.make_async_copy(kinds_any, kinds_ref, sems.at[1]),
    ]
    for copy in copies:
        copy.start()
    rows, per_row, proj, tile = tiles_ref.shape
    points = rows * tile
    groups = columns_ref.shape[1] // points
    bands = groups * columns_ref.shape[0]
    depth = per_row * proj
    total[...] = jnp.zeros_like(total)

    def products(step):
        columns = jnp.concatenate(
            [
                columns_ref[:, pl.ds(pl.multiple_of(g * points + (step * 2 + row) * tile, tile), tile)]
                for row in range(2)
                for g in range(groups)
            ],
            axis=0,
        )
        values = tiles_ref[pl.ds(step * 2, 2)].reshape(2 * depth, tile)
        part = lax.dot_general(
            values, columns, (((1,), (1,)), ((), ())), preferred_element_type=jnp.float32
        )
        return part[:depth, :bands], part[depth:, bands:]

    def add(r, part):
        for j in range(per_row):
            total[slot_of(names_ref, r, j)] += part[j * proj : (j + 1) * proj]

    def pair(step, carry):
        for row, part in enumerate(products(step)):
            add(step * 2 + row, part)
        return carry

    ahead = early.shape[0] // 2
    for step in range(ahead):
        for row, part in enumerate(products(step)):
            early[step * 2 + row] = part
    for copy in copies:
        copy.wait()
    for r in range(2 * ahead):
        add(r, early[r])
    lax.fori_loop(ahead, rows // 2, pair, 0, unroll=rows // 2 - ahead)
    own_ref[...] = total[EDGE:].reshape(own_ref.shape)
    edge_ref[...] = total[0].astype(edge_ref.dtype)
    for atom in range(kinds_ref.shape[0]):
        matrices_ref[atom] = couplings_ref[kinds_ref[atom]]


def share_kernel(own_ref, later_ref, shared_ref):
    last = own_ref.shape[0] - later_ref.shape[0]
    kept = own_ref[:last].astype(shared_ref.dtype)
    summed = (own_ref[last:] + later_ref[...].astype(jnp.float32)).astype(shared_ref.dtype)
    for target in range(shared_ref.shape[0]):
        shared_ref[target, :last] = kept
        shared_ref[target, last:] = summed


def couple_kernel(parts_ref, matrices_ref, coupled_ref):
    atoms, width, _ = matrices_ref.shape
    summed = parts_ref[0].astype(jnp.float32)
    for source in range(1, parts_ref.shape[0]):
        summed = summed + parts_ref[source].astype(jnp.float32)
    for atom in range(atoms):
        at = slice(atom * width, (atom + 1) * width)
        coupled_ref[at] = jnp.dot(
            matrices_ref[atom],
            summed[at],
            precision=lax.Precision.HIGHEST,
            preferred_element_type=jnp.float32,
        ).astype(coupled_ref.dtype)


def backward_kernel(
    order, names_any, earlier_ref, coupled_ref, tiles_ref, out_ref, pairs, names_ref, sem
):
    copy = pltpu.make_async_copy(names_any, names_ref, sem)
    copy.start()
    rows, per_row, proj, tile = tiles_ref.shape
    points = rows * tile
    groups = out_ref.shape[1] // points
    local = out_ref.shape[0]
    blocks = [earlier_ref[...]] + [coupled_ref[k * proj : (k + 1) * proj] for k in range(BLK)]
    blocks = [b.astype(jnp.float32) for b in blocks]
    for first in range(SLOTS):
        for second in range(SLOTS):
            both = jnp.concatenate([blocks[first], blocks[second]], axis=0)
            pairs[first * SLOTS + second] = both.T.astype(pairs.dtype)
    copy.wait()

    def row(r, carry):
        values = tiles_ref[r].reshape(per_row * proj, tile)
        chosen = pairs[slot_of(names_ref, r, 0) * SLOTS + slot_of(names_ref, r, 1)]
        result = jnp.dot(chosen, values, preferred_element_type=jnp.float32)
        result = result.astype(out_ref.dtype)
        for g in range(groups):
            at = pl.ds(pl.multiple_of(order.index(g) * points + r * tile, tile), tile)
            out_ref[:, at] = result[g * local : (g + 1) * local]
        return carry

    lax.fori_loop(0, rows, row, 0, unroll=rows)


def place_kernel(order, blocks_ref, out_any, sems):
    width = blocks_ref.shape[1] // len(order)
    copies = [
        pltpu.make_async_copy(
            blocks_ref.at[:, pl.ds(k * width, width)],
            out_any.at[:, pl.ds(device * width, width)],
            sems.at[k],
        )
        for k, device in enumerate(order)
    ]
    for copy in copies:
        copy.start()
    for copy in copies:
        copy.wait()


def from_behind(block, axis, distance):
    size = lax.axis_size(axis)
    return lax.ppermute(block, axis, [(i, (i + distance) % size) for i in range(size)])


def body(psi, tiles, tile_block, couplings, species):
    splits = lax.axis_size("grid")
    local_bands = psi.shape[0]
    rows, per_row, tile, proj = tiles.shape
    bands = local_bands * splits
    points = rows * tile
    flops = 2 * rows * per_row * proj * tile * bands
    moved = 2 * (bands * points + tiles.size)
    last = (BLK - EDGE) * proj
    names = tile_block.T
    order = [i ^ (i >> 1) for i in range(splits)]
    order = order[splits // 2 :] + order[: splits // 2]
    values = jnp.transpose(tiles, (0, 1, 3, 2))

    spread = lax.all_to_all(psi, "grid", split_axis=1, concat_axis=1, tiled=True)
    own, edge, matrices = call(
        forward_kernel,
        (
            jax.ShapeDtypeStruct((BLK * proj, bands), jnp.float32),
            jax.ShapeDtypeStruct((proj, bands), jnp.bfloat16),
            jax.ShapeDtypeStruct(species.shape + couplings.shape[1:], jnp.float32),
        ),
        (pl.ANY, pl.ANY, pltpu.VMEM, pltpu.VMEM, pltpu.VMEM),
        (pltpu.VMEM, pltpu.VMEM, pltpu.VMEM),
        [
            pltpu.VMEM((SLOTS, proj, bands), jnp.float32),
            pltpu.VMEM((2 * AHEAD, per_row * proj, bands), jnp.float32),
            pltpu.SMEM(names.shape, jnp.int32),
            pltpu.SMEM(species.shape, jnp.int32),
            pltpu.SemaphoreType.DMA((2,)),
        ],
        flops,
        moved,
    )(names, species, spread, values, couplings)
    later = from_behind(edge, "band", -1)
    shared = call(
        share_kernel,
        jax.ShapeDtypeStruct((splits,) + own.shape, jnp.bfloat16),
        (pltpu.VMEM, pltpu.VMEM),
        pltpu.VMEM,
    )(own, later)
    parts = lax.all_to_all(shared, "grid", split_axis=0, concat_axis=0, tiled=True)
    coupled = call(
        couple_kernel,
        jax.ShapeDtypeStruct((BLK * proj, bands), jnp.bfloat16),
        (pltpu.VMEM, pltpu.VMEM),
        pltpu.VMEM,
    )(parts, matrices)
    earlier = from_behind(coupled[last:], "band", 1)
    result = call(
        functools.partial(backward_kernel, order),
        jax.ShapeDtypeStruct(psi.shape, jnp.bfloat16),
        (pl.ANY, pltpu.VMEM, pltpu.VMEM, pltpu.VMEM),
        pltpu.VMEM,
        [
            pltpu.VMEM((SLOTS * SLOTS, bands, per_row * proj), jnp.bfloat16),
            pltpu.SMEM(names.shape, jnp.int32),
            pltpu.SemaphoreType.DMA(()),
        ],
        flops,
        moved,
    )(names, earlier, coupled, values)
    returned = lax.all_to_all(
        result, "grid", split_axis=1, concat_axis=1, tiled=True, axis_index_groups=[order]
    )
    return call(
        functools.partial(place_kernel, order),
        jax.ShapeDtypeStruct(psi.shape, jnp.bfloat16),
        (pltpu.VMEM,),
        pl.ANY,
        [pltpu.SemaphoreType.DMA((splits,))],
    )(returned)


def solution(mesh):
    return jax.shard_map(
        body,
        mesh=mesh,
        in_specs=(
            P("grid", "band"),
            P(("band", "grid"), None, None, None),
            P(("band", "grid"), None),
            P(),
            P("band"),
        ),
        out_specs=P("grid", "band"),
        check_vma=False,
    )
```
